512 devices in a mesh: seq: 16 (over z, core), grp: 32 (over x, y).
Axes of the slice: x: 4, y: 8, z: 8, core: 2. Of those that a mesh axis runs over, the one named last changes fastest.
Arguments:
- post_gate: bfloat16 [2048, 8192], P('seq', 'grp'), may hold values from -6 to 6
- pre_gate: bfloat16 [2048, 8192], P('seq', 'grp'), may hold values from -6 to 6
- values_in: bfloat16 [2048, 8192], P('seq', 'grp'), may hold values from -6 to 6
- filters: bfloat16 [512, 2048], P('grp'), may hold values from -1 to 1
- grad_out: bfloat16 [2048, 8192], P('seq', 'grp'), may hold values from -6 to 6
Outputs:
- output: bfloat16 [2048, 8192], P('seq', 'grp')
- grad_post: bfloat16 [2048, 8192], P('seq', 'grp')
- grad_pre: bfloat16 [2048, 8192], P('seq', 'grp')
- grad_values: bfloat16 [2048, 8192], P('seq', 'grp')
- grad_filters: float32 [512, 2048], P('grp', 'seq')
The draws below stay inside these ranges and needn't reach their ends.
All inputs are finite; a program needn't handle non-finite values.
Results may differ from the reference program's by a relative error of at most 0.0049.
Values may be sent and summed in bfloat16 or wider, within the bound.
No kernel may reach another device: no remote copies, remote signals or barrier semaphores. Data moves between devices by JAX's collectives and lax.ppermute only.
A program may use at most 64 MiB of HBM per device.

```python
import math
import jax
import jax.numpy as jnp
from jax import lax

D = 8192
GROUP = 16
LENGTH = 2048
FGROUPS = 512


def draw_filters(key, part):
    key = jax.random.fold_in(key, 11)
    decay_key, jitter_key = jax.random.split(key)
    lag_index = jnp.arange(LENGTH, dtype=jnp.float32)[None, :]
    log_decay = jax.random.uniform(decay_key, (FGROUPS, 1), jnp.float32, math.log(0.5 / LENGTH), math.log(1.0 / 40.0))
    jitter = jax.random.truncated_normal(jitter_key, -4.0, 4.0, (FGROUPS, LENGTH), jnp.float32)
    decays = jnp.exp(log_decay)
    envelope = jnp.exp(-lag_index * decays) * jnp.sqrt(1.0 - jnp.exp(-2.0 * decays))
    return (jitter * envelope).astype(jnp.bfloat16)


def shard_levels(rng, extent, pieces, smallest, high):
    def one(axis_at, parts):
        steps = jax.random.uniform(jax.random.fold_in(jax.random.fold_in(rng, 6), axis_at), (parts,), jnp.float32, smallest / len(pieces), high / len(pieces))
        return jnp.repeat(jnp.exp(steps), extent[axis_at] // parts).reshape((-1,) + (1,) * (len(extent) - axis_at - 1))

    loudness = one(*pieces[0])
    for cut in pieces[1:]:
        loudness = loudness * one(*cut)
    return loudness


def scatter_about(rng, extent, deviation, limit, shards=(), kind=jnp.bfloat16):
    values = jax.random.normal(rng, extent, jnp.float32) * deviation
    if len(shards) > 0:
        values = shard_levels(rng, extent, shards, -0.22, 0.18) * values
    return jnp.clip(values, min=-limit, max=limit).astype(kind)


def setup_inputs(seed: int = 0) -> dict:
    splits = jax.random.split(jax.random.key(seed), 6)
    return {
        "post_gate": scatter_about(splits[0], (LENGTH, D), 1.0, 6.0, ((0, 16), (1, 32))),
        "pre_gate": scatter_about(splits[1], (LENGTH, D), 1.0, 6.0, ((0, 16), (1, 32))),
        "values_in": scatter_about(splits[2], (LENGTH, D), 1.0, 6.0, ((0, 16), (1, 32))),
        "filters": draw_filters(jax.random.fold_in(splits[5], 71), 0),
        "grad_out": scatter_about(splits[4], (LENGTH, D), 1.0, 6.0, ((0, 16), (1, 32))),
    }


def reference(post_gate, pre_gate, values_in, filters, grad_out):
    length = post_gate.shape[0]
    channels = post_gate.shape[1]
    mixed_in = (pre_gate.astype(jnp.float32) * values_in.astype(jnp.float32)).astype(jnp.bfloat16)
    grad_mix = (grad_out.astype(jnp.float32) * post_gate.astype(jnp.float32)).astype(jnp.bfloat16)
    period = 2 * length
    spec_in = jnp.fft.rfft(mixed_in.astype(jnp.float32), period, axis=0)
    spec_grad = jnp.fft.rfft(grad_mix.astype(jnp.float32), period, axis=0)
    spec_filter = jnp.fft.rfft(filters.astype(jnp.float32).T, period, axis=0)
    n_bins = spec_in.shape[0]
    grouped_in = spec_in.reshape(n_bins, FGROUPS, GROUP)
    grouped_grad = spec_grad.reshape(n_bins, FGROUPS, GROUP)
    filt_spec = (grouped_in * spec_filter[:, :, None]).reshape(n_bins, channels)
    filtered = jnp.fft.irfft(filt_spec, period, axis=0)[:length].astype(jnp.float32)
    back_spec = (grouped_grad * jnp.conj(spec_filter)[:, :, None]).reshape(n_bins, channels)
    grad_mixed = jnp.fft.irfft(back_spec, period, axis=0)[:length].astype(jnp.float32)
    cross = lax.optimization_barrier(jnp.sum(grouped_grad * jnp.conj(grouped_in), axis=2))
    lag_grad = jnp.fft.irfft(cross, period, axis=0)[:length].T.astype(jnp.float32)
    grad_scale = 1.0 / jnp.sqrt(jnp.float32(GROUP * LENGTH))
    output = (post_gate.astype(jnp.float32) * filtered).astype(jnp.bfloat16)
    grad_post = (grad_out.astype(jnp.float32) * filtered).astype(jnp.bfloat16)
    grad_pre = (grad_mixed * values_in.astype(jnp.float32)).astype(jnp.bfloat16)
    grad_values = (grad_mixed * pre_gate.astype(jnp.float32)).astype(jnp.bfloat16)
    return (output, grad_post, grad_pre, grad_values, lag_grad * grad_scale)
```

```python
import functools
import math

import jax
import jax.numpy as jnp
from jax import lax
from jax.experimental import pallas as pl
from jax.experimental.pallas import tpu as pltpu
from jax.sharding import PartitionSpec as P

GROUP = 16
F32 = jnp.float32
BF16 = jnp.bfloat16


def pack_kernel(post_ref, pre_ref, values_ref, gout_ref, send_ref):
    n_filters = send_ref.shape[0]
    tokens = post_ref.shape[0]
    mixed = pre_ref[...].astype(F32) * values_ref[...].astype(F32)
    grads = gout_ref[...].astype(F32) * post_ref[...].astype(F32)
    send_ref[:, 0:GROUP, :] = mixed.astype(BF16).T.reshape(n_filters, GROUP, tokens)
    send_ref[:, GROUP : 2 * GROUP, :] = grads.astype(BF16).T.reshape(n_filters, GROUP, tokens)


def conv_kernel(own_ref, recv_ref, filters_ref, back_ref):
    blocks, _, width = recv_ref.shape
    rows = blocks * GROUP
    length = blocks * width
    xt = recv_ref[:, 0:GROUP, :].reshape(rows, width)
    gt = recv_ref[:, GROUP : 2 * GROUP, :].reshape(rows, width)
    own = own_ref[0]
    taps = filters_ref[...].astype(F32)
    which = lax.broadcasted_iota(jnp.int32, taps.shape, 0)
    row = jnp.sum(jnp.where(which == own, taps, 0.0), axis=0, keepdims=True)
    padded = jnp.concatenate([jnp.zeros((1, width), F32), row], axis=1)
    toep = pltpu.roll(
        jnp.broadcast_to(padded, (width, length + width)), 0, 1, stride=1, stride_axis=0
    ).astype(BF16)

    filt = None
    back = None
    for d in range(blocks):
        kern = toep[:, width * (d + 1) : width * (d + 2)]
        part = jnp.dot(xt[: rows - GROUP * d], kern, preferred_element_type=F32)
        rev = lax.dot_general(
            gt[GROUP * d :], kern, (((1,), (1,)), ((), ())), preferred_element_type=F32
        )
        if d == 0:
            filt, back = part, rev
        else:
            zeros = jnp.zeros((GROUP * d, width), F32)
            filt = filt + jnp.concatenate([zeros, part], axis=0)
            back = back + jnp.concatenate([rev, zeros], axis=0)
    back_ref[:, 0:GROUP, :] = filt.astype(BF16).reshape(blocks, GROUP, width)
    back_ref[:, GROUP : 2 * GROUP, :] = back.astype(BF16).reshape(blocks, GROUP, width)

    at = lax.broadcasted_iota(jnp.int32, (width, width), 0)
    to = lax.broadcasted_iota(jnp.int32, (width, width), 1)
    flip = jnp.where(at + to == width - 1, 1.0, 0.0).astype(BF16)
    x_rev = lax.dot_general(
        flip, xt, (((1,), (1,)), ((), ())), preferred_element_type=F32
    ).astype(BF16)
    gt_pad = jnp.concatenate([gt, jnp.zeros((rows, width), BF16)], axis=0)
    pairs = [
        jnp.dot(x_rev, gt_pad[GROUP * d : GROUP * d + rows], preferred_element_type=F32)
        for d in range(blocks)
    ]
    pairs = jnp.concatenate(pairs + [jnp.zeros((width, width), F32)], axis=1)
    turned = pltpu.roll(pairs, 1, 1, stride=1, stride_axis=0)
    lags = jnp.sum(turned[:, width:], axis=0, keepdims=True)
    high = lags.astype(BF16).astype(F32)
    rest = lags - high
    mid = rest.astype(BF16).astype(F32)
    low = rest - mid
    terms = jnp.concatenate([high, mid, low, jnp.zeros((13, length), F32)], axis=0).astype(BF16)
    for i in range(blocks):
        back_ref[i, 2 * GROUP : 3 * GROUP, :] = terms[:, width * i : width * (i + 1)]


def gate_kernel(length, recv_ref, post_ref, pre_ref, values_ref, gout_ref, out_ref, gpost_ref, gpre_ref, gval_ref, gfilt_ref):
    n_filters, _, tokens = recv_ref.shape
    channels = n_filters * GROUP
    filt = recv_ref[:, 0:GROUP, :].reshape(channels, tokens).astype(F32).T
    back = recv_ref[:, GROUP : 2 * GROUP, :].reshape(channels, tokens).astype(F32).T
    out_ref[...] = (post_ref[...].astype(F32) * filt).astype(BF16)
    gpost_ref[...] = (gout_ref[...].astype(F32) * filt).astype(BF16)
    gpre_ref[...] = (back * values_ref[...].astype(F32)).astype(BF16)
    gval_ref[...] = (back * pre_ref[...].astype(F32)).astype(BF16)
    scale = 1.0 / math.sqrt(GROUP * length)
    terms = recv_ref[:, 2 * GROUP : 3 * GROUP, :].astype(F32)
    gfilt_ref[...] = jnp.sum(terms, axis=1) * scale


def on_device(post_gate, pre_gate, values_in, filters, grad_out):
    tokens, channels = post_gate.shape
    n_filters, length = filters.shape
    vmem = pl.BlockSpec(memory_space=pltpu.VMEM)
    smem = pl.BlockSpec(memory_space=pltpu.SMEM)
    send = pl.pallas_call(
        pack_kernel,
        out_shape=jax.ShapeDtypeStruct((n_filters, 2 * GROUP, tokens), BF16),
        in_specs=[vmem] * 4,
        out_specs=vmem,
        name="pack",
    )(post_gate, pre_gate, values_in, grad_out)
    recv = lax.all_to_all(send, "seq", 0, 0, tiled=True)
    own = lax.axis_index("seq").astype(jnp.int32).reshape(1)
    back = pl.pallas_call(
        conv_kernel,
        out_shape=jax.ShapeDtypeStruct((n_filters, 3 * GROUP, tokens), BF16),
        in_specs=[smem, vmem, vmem],
        out_specs=vmem,
        name="conv",
    )(own, recv, filters)
    back = lax.all_to_all(back, "seq", 0, 0, tiled=True)
    grid_out = jax.ShapeDtypeStruct((tokens, channels), BF16)
    return pl.pallas_call(
        functools.partial(gate_kernel, length),
        out_shape=(grid_out,) * 4 + (jax.ShapeDtypeStruct((n_filters, tokens), F32),),
        in_specs=[vmem] * 5,
        out_specs=(vmem,) * 5,
        name="gate",
    )(back, post_gate, pre_gate, values_in, grad_out)


def solution(mesh):
    return jax.shard_map(
        on_device,
        mesh=mesh,
        in_specs=(
            P("seq", "grp"),
            P("seq", "grp"),
            P("seq", "grp"),
            P("grp", None),
            P("seq", "grp"),
        ),
        out_specs=(
            P("seq", "grp"),
            P("seq", "grp"),
            P("seq", "grp"),
            P("seq", "grp"),
            P("grp", "seq"),
        ),
        check_vma=False,
    )
```

```python
import functools
import math

import jax
import jax.numpy as jnp
from jax import lax
from jax.experimental import pallas as pl
from jax.experimental.pallas import tpu as pltpu
from jax.sharding import PartitionSpec as P

GROUP = 16
F32 = jnp.float32
BF16 = jnp.bfloat16
VMEM = 8 * 1024 * 1024


def pack_kernel(post_hbm, pre_hbm, values_hbm, gout_hbm, send_ref, held, sems):
    n_filters, _, tokens = send_ref.shape
    copies = [
        pltpu.make_async_copy(hbm, held.at[k], sems.at[k])
        for k, hbm in enumerate((pre_hbm, values_hbm, gout_hbm, post_hbm))
    ]
    for copy in copies:
        copy.start()
    for k in range(2):
        copies[2 * k].wait()
        copies[2 * k + 1].wait()
        product = held[2 * k].astype(F32) * held[2 * k + 1].astype(F32)
        send_ref[:, GROUP * k : GROUP * (k + 1), :] = product.astype(BF16).T.reshape(
            n_filters, GROUP, tokens
        )


def conv_kernel(recv_ref, filters_ref, back_ref):
    blocks, _, width = recv_ref.shape
    rows = blocks * GROUP
    length = blocks * width
    xt = recv_ref[:, 0:GROUP, :].reshape(rows, width)
    gt = recv_ref[:, GROUP : 2 * GROUP, :].reshape(rows, width)
    own = lax.axis_index("seq")
    taps = filters_ref[...].astype(F32)
    which = lax.broadcasted_iota(jnp.int32, taps.shape, 0)
    row = jnp.sum(jnp.where(which == own, taps, 0.0), axis=0, keepdims=True)
    padded = jnp.concatenate([jnp.zeros((1, width), F32), row], axis=1)
    toep = pltpu.roll(
        jnp.broadcast_to(padded, (width, length + width)), 0, 1, stride=1, stride_axis=0
    ).astype(BF16)

    filt = None
    back = None
    for d in range(blocks):
        kern = toep[:, width * (d + 1) : width * (d + 2)]
        part = jnp.dot(xt[: rows - GROUP * d], kern, preferred_element_type=F32)
        rev = lax.dot_general(
            gt[GROUP * d :], kern, (((1,), (1,)), ((), ())), preferred_element_type=F32
        )
        if d == 0:
            filt, back = part, rev
        else:
            zeros = jnp.zeros((GROUP * d, width), F32)
            filt = filt + jnp.concatenate([zeros, part], axis=0)
            back = back + jnp.concatenate([rev, zeros], axis=0)
    back_ref[:, 0:GROUP, :] = filt.astype(BF16).reshape(blocks, GROUP, width)
    back_ref[:, GROUP : 2 * GROUP, :] = back.astype(BF16).reshape(blocks, GROUP, width)

    at = lax.broadcasted_iota(jnp.int32, (width, width), 0)
    to = lax.broadcasted_iota(jnp.int32, (width, width), 1)
    flip = jnp.where(at + to == width - 1, 1.0, 0.0).astype(BF16)
    x_rev = lax.dot_general(
        flip, xt, (((1,), (1,)), ((), ())), preferred_element_type=F32
    ).astype(BF16)
    gt_pad = jnp.concatenate([gt, jnp.zeros((rows, width), BF16)], axis=0)
    pairs = [
        jnp.dot(x_rev, gt_pad[GROUP * d : GROUP * d + rows], preferred_element_type=F32)
        for d in range(blocks)
    ]
    pairs = jnp.concatenate(pairs + [jnp.zeros((width, width), F32)], axis=1)
    turned = pltpu.roll(pairs, 1, 1, stride=1, stride_axis=0)
    lags = jnp.sum(turned[:, width:], axis=0, keepdims=True)
    high = lags.astype(BF16).astype(F32)
    rest = lags - high
    mid = rest.astype(BF16).astype(F32)
    low = rest - mid
    terms = jnp.concatenate([high, mid, low, jnp.zeros((13, length), F32)], axis=0).astype(BF16)
    for i in range(blocks):
        back_ref[i, 2 * GROUP : 3 * GROUP, :] = terms[:, width * i : width * (i + 1)]


def gate_kernel(length, recv_ref, post_ref, pre_ref, values_ref, gout_ref, out_ref, gpost_ref, gpre_ref, gval_ref, gfilt_ref):
    n_filters, _, tokens = recv_ref.shape
    channels = n_filters * GROUP
    filt = recv_ref[:, 0:GROUP, :].reshape(channels, tokens).astype(F32).T
    back = recv_ref[:, GROUP : 2 * GROUP, :].reshape(channels, tokens).astype(F32).T
    out_ref[...] = (post_ref[...].astype(F32) * filt).astype(BF16)
    gpost_ref[...] = (gout_ref[...].astype(F32) * filt).astype(BF16)
    gpre_ref[...] = (back * values_ref[...].astype(F32)).astype(BF16)
    gval_ref[...] = (back * pre_ref[...].astype(F32)).astype(BF16)
    scale = 1.0 / math.sqrt(GROUP * length)
    terms = recv_ref[:, 2 * GROUP : 3 * GROUP, :].astype(F32)
    gfilt_ref[...] = jnp.sum(terms, axis=1) * scale


def on_device(post_gate, pre_gate, values_in, filters, grad_out):
    tokens, channels = post_gate.shape
    n_filters, length = filters.shape
    vmem = pl.BlockSpec(memory_space=pltpu.VMEM)
    hbm = pl.BlockSpec(memory_space=pltpu.HBM)
    send = pl.pallas_call(
        pack_kernel,
        out_shape=jax.ShapeDtypeStruct((n_filters, 2 * GROUP, tokens), BF16),
        in_specs=[hbm] * 4,
        out_specs=vmem,
        scratch_shapes=[
            pltpu.VMEM((4, tokens, channels), BF16),
            pltpu.SemaphoreType.DMA((4,)),
        ],
        compiler_params=pltpu.CompilerParams(vmem_limit_bytes=VMEM),
        name="pack",
    )(*[pltpu.with_memory_space_constraint(x, pltpu.HBM) for x in (post_gate, pre_gate, values_in, grad_out)])
    recv = lax.all_to_all(send, "seq", 0, 0, tiled=True)
    back = pl.pallas_call(
        conv_kernel,
        out_shape=jax.ShapeDtypeStruct((n_filters, 3 * GROUP, tokens), BF16),
        in_specs=[vmem, vmem],
        out_specs=vmem,
        compiler_params=pltpu.CompilerParams(vmem_limit_bytes=VMEM),
        name="conv",
    )(recv, filters)
    back = lax.all_to_all(back, "seq", 0, 0, tiled=True)
    grid_out = jax.ShapeDtypeStruct((tokens, channels), BF16)
    return pl.pallas_call(
        functools.partial(gate_kernel, length),
        out_shape=(grid_out,) * 4 + (jax.ShapeDtypeStruct((n_filters, tokens), F32),),
        in_specs=[vmem] * 5,
        out_specs=(vmem,) * 5,
        compiler_params=pltpu.CompilerParams(vmem_limit_bytes=VMEM),
        name="gate",
    )(back, post_gate, pre_gate, values_in, grad_out)


def solution(mesh):
    return jax.shard_map(
        on_device,
        mesh=mesh,
        in_specs=(
            P("seq", "grp"),
            P("seq", "grp"),
            P("seq", "grp"),
            P("grp", None),
            P("seq", "grp"),
        ),
        out_specs=(
            P("seq", "grp"),
            P("seq", "grp"),
            P("seq", "grp"),
            P("seq", "grp"),
            P("grp", "seq"),
        ),
        check_vma=False,
    )
```

```python
import functools
import math

import jax
import jax.numpy as jnp
from jax import lax
from jax.experimental import pallas as pl
from jax.experimental.pallas import tpu as pltpu
from jax.sharding import PartitionSpec as P

GROUP = 16
BACK_ROWS = 2 * GROUP + 8
F32 = jnp.float32
BF16 = jnp.bfloat16
VMEM = 8 * 1024 * 1024


ORDER_IN = list(range(15, -1, -1))
ORDER_OUT = list(range(0, 16, 2)) + list(range(1, 16, 2))


def pack_kernel(post_hbm, pre_hbm, values_hbm, gout_hbm, send_ref, held, sems):
    copies = [
        pltpu.make_async_copy(hbm, held.at[k], sems.at[k])
        for k, hbm in enumerate((pre_hbm, values_hbm, gout_hbm, post_hbm))
    ]
    for copy in copies:
        copy.start()
    for k in range(2):
        copies[2 * k].wait()
        copies[2 * k + 1].wait()
        product = held[2 * k].astype(F32) * held[2 * k + 1].astype(F32)
        turned = product.astype(BF16).T
        for place, f in enumerate(ORDER_IN):
            send_ref[place, GROUP * k : GROUP * (k + 1), :] = turned[GROUP * f : GROUP * (f + 1)]


def conv_kernel(recv_ref, filters_ref, back_ref):
    blocks, _, width = recv_ref.shape
    rows = blocks * GROUP
    length = blocks * width
    places = [ORDER_IN.index(block) for block in range(blocks)]
    xt = jnp.concatenate([recv_ref[p, 0:GROUP, :] for p in places], axis=0)
    gt = jnp.concatenate([recv_ref[p, GROUP : 2 * GROUP, :] for p in places], axis=0)
    own = lax.axis_index("seq")
    taps = filters_ref[...].astype(F32)
    which = lax.broadcasted_iota(jnp.int32, taps.shape, 0)
    row = jnp.sum(jnp.where(which == own, taps, 0.0), axis=0, keepdims=True)
    padded = jnp.concatenate([jnp.zeros((1, width), F32), row], axis=1)
    toep = pltpu.roll(
        jnp.broadcast_to(padded, (width, length + width)), 0, 1, stride=1, stride_axis=0
    ).astype(BF16)

    def wide(v):
        v = v.reshape(blocks // 2, 2, GROUP, width)
        return jnp.concatenate([v[:, 0].reshape(half, width), v[:, 1].reshape(half, width)], axis=1)

    half = rows // 2
    x2 = wide(xt)
    g2 = wide(gt)
    filt2 = None
    back2 = None
    for d in range(blocks // 2):
        top = toep[:, width * (2 * d + 1) : width * (2 * d + 3)]
        if d == 0:
            low = jnp.concatenate([jnp.zeros((width, width), BF16), toep[:, width : 2 * width]], axis=1)
        else:
            low = toep[:, width * 2 * d : width * (2 * d + 2)]
        kern = jnp.concatenate([top, low], axis=0)
        part = jnp.dot(x2[: half - GROUP * d], kern, preferred_element_type=F32)
        rev = lax.dot_general(
            g2[GROUP * d :], kern, (((1,), (1,)), ((), ())), preferred_element_type=F32
        )
        if d == 0:
            filt2, back2 = part, rev
        else:
            zeros = jnp.zeros((GROUP * d, 2 * width), F32)
            filt2 = filt2 + jnp.concatenate([zeros, part], axis=0)
            back2 = back2 + jnp.concatenate([rev, zeros], axis=0)
    filt2 = filt2.astype(BF16)
    back2 = back2.astype(BF16)
    for place, i in enumerate(ORDER_OUT):
        at = (slice(GROUP * (i // 2), GROUP * (i // 2 + 1)), slice(width * (i % 2), width * (i % 2 + 1)))
        back_ref[place, 0:GROUP, :] = filt2[at]
        back_ref[place, GROUP : 2 * GROUP, :] = back2[at]

    at = lax.broadcasted_iota(jnp.int32, (width, width), 0)
    to = lax.broadcasted_iota(jnp.int32, (width, width), 1)
    flip = jnp.where(at + to == width - 1, 1.0, 0.0).astype(BF16)
    x_rev = lax.dot_general(
        flip, xt, (((1,), (1,)), ((), ())), preferred_element_type=F32
    ).astype(BF16)
    gt_pad = jnp.concatenate([gt, jnp.zeros((rows, width), BF16)], axis=0)
    pairs = [
        jnp.dot(
            x_rev,
            jnp.concatenate(
                [gt_pad[GROUP * d : GROUP * d + rows], gt_pad[GROUP * (d + 1) : GROUP * (d + 1) + rows]],
                axis=1,
            ),
            preferred_element_type=F32,
        )
        for d in range(0, blocks, 2)
    ]
    pairs = jnp.concatenate(pairs + [jnp.zeros((width, width), F32)], axis=1)
    turned = pltpu.roll(pairs, 1, 1, stride=1, stride_axis=0)
    lags = jnp.sum(turned[:, width:], axis=0, keepdims=True)
    high = lags.astype(BF16).astype(F32)
    rest = lags - high
    mid = rest.astype(BF16).astype(F32)
    low = rest - mid
    terms = jnp.concatenate([high, mid, low, jnp.zeros((5, length), F32)], axis=0).astype(BF16)
    for place, i in enumerate(ORDER_OUT):
        back_ref[place, 2 * GROUP : BACK_ROWS, :] = terms[:, width * i : width * (i + 1)]


def gate_kernel(length, recv_ref, post_ref, pre_ref, values_ref, gout_ref, out_ref, gpost_ref, gpre_ref, gval_ref, gfilt_ref):
    n_filters = recv_ref.shape[0]
    places = [ORDER_OUT.index(f) for f in range(n_filters)]
    filt = jnp.concatenate([recv_ref[p, 0:GROUP, :] for p in places], axis=0).astype(F32).T
    back = jnp.concatenate([recv_ref[p, GROUP : 2 * GROUP, :] for p in places], axis=0).astype(F32).T
    out_ref[...] = (post_ref[...].astype(F32) * filt).astype(BF16)
    gpost_ref[...] = (gout_ref[...].astype(F32) * filt).astype(BF16)
    gpre_ref[...] = (back * values_ref[...].astype(F32)).astype(BF16)
    gval_ref[...] = (back * pre_ref[...].astype(F32)).astype(BF16)
    scale = 1.0 / math.sqrt(GROUP * length)
    lags = [
        jnp.sum(recv_ref[p, 2 * GROUP : BACK_ROWS, :].astype(F32), axis=0, keepdims=True)
        for p in places
    ]
    gfilt_ref[...] = jnp.concatenate(lags, axis=0) * scale


def on_device(post_gate, pre_gate, values_in, filters, grad_out):
    tokens, channels = post_gate.shape
    n_filters, length = filters.shape
    vmem = pl.BlockSpec(memory_space=pltpu.VMEM)
    hbm = pl.BlockSpec(memory_space=pltpu.HBM)
    send = pl.pallas_call(
        pack_kernel,
        out_shape=jax.ShapeDtypeStruct((n_filters, 2 * GROUP, tokens), BF16),
        in_specs=[hbm] * 4,
        out_specs=vmem,
        scratch_shapes=[
            pltpu.VMEM((4, tokens, channels), BF16),
            pltpu.SemaphoreType.DMA((4,)),
        ],
        compiler_params=pltpu.CompilerParams(vmem_limit_bytes=VMEM),
        name="pack",
    )(*[pltpu.with_memory_space_constraint(x, pltpu.HBM) for x in (post_gate, pre_gate, values_in, grad_out)])
    recv = lax.all_to_all(
        send, "seq", 0, 0, tiled=True, axis_index_groups=[ORDER_IN]
    )
    back = pl.pallas_call(
        conv_kernel,
        out_shape=jax.ShapeDtypeStruct((n_filters, BACK_ROWS, tokens), BF16),
        in_specs=[vmem, vmem],
        out_specs=vmem,
        compiler_params=pltpu.CompilerParams(vmem_limit_bytes=VMEM),
        name="conv",
    )(recv, filters)
    back = lax.all_to_all(
        back, "seq", 0, 0, tiled=True, axis_index_groups=[ORDER_OUT]
    )
    grid_out = jax.ShapeDtypeStruct((tokens, channels), BF16)
    return pl.pallas_call(
        functools.partial(gate_kernel, length),
        out_shape=(grid_out,) * 4 + (jax.ShapeDtypeStruct((n_filters, tokens), F32),),
        in_specs=[vmem] * 5,
        out_specs=(vmem,) * 5,
        compiler_params=pltpu.CompilerParams(vmem_limit_bytes=VMEM),
        name="gate",
    )(back, post_gate, pre_gate, values_in, grad_out)


def solution(mesh):
    return jax.shard_map(
        on_device,
        mesh=mesh,
        in_specs=(
            P("seq", "grp"),
            P("seq", "grp"),
            P("seq", "grp"),
            P("grp", None),
            P("seq", "grp"),
        ),
        out_specs=(
            P("seq", "grp"),
            P("seq", "grp"),
            P("seq", "grp"),
            P("seq", "grp"),
            P("grp", "seq"),
        ),
        check_vma=False,
    )
```

```python
import functools
import math

import jax
import jax.numpy as jnp
from jax import lax
from jax.experimental import pallas as pl
from jax.experimental.pallas import tpu as pltpu
from jax.sharding import PartitionSpec as P

GROUP = 16
BACK_PAIRS = GROUP + 1
F32 = jnp.float32
BF16 = jnp.bfloat16
VMEM = 8 * 1024 * 1024


ORDER_IN = [13, 11, 9, 7, 5, 3, 1, 15, 12, 10, 8, 6, 4, 2, 0, 14]
ORDER_OUT = [13, 15, 0, 2, 4, 6, 8, 10, 12, 14, 1, 3, 5, 7, 9, 11]


def pack_kernel(post_hbm, pre_hbm, values_hbm, gout_hbm, send_ref, held, sems):
    copies = [
        pltpu.make_async_copy(hbm, held.at[k], sems.at[k])
        for k, hbm in enumerate((pre_hbm, values_hbm, gout_hbm, post_hbm))
    ]
    for copy in copies:
        copy.start()
    for k in range(2):
        copies[2 * k].wait()
        copies[2 * k + 1].wait()
        product = held[2 * k].astype(F32) * held[2 * k + 1].astype(F32)
        turned = product.astype(BF16).T
        for place, f in enumerate(ORDER_IN):
            send_ref[place, GROUP * k : GROUP * (k + 1), :] = turned[GROUP * f : GROUP * (f + 1)]


def conv_kernel(recv_ref, filters_ref, back_ref):
    blocks, _, width = recv_ref.shape
    rows = blocks * GROUP
    length = blocks * width
    places = [ORDER_IN.index(block) for block in range(blocks)]
    xt = jnp.concatenate([recv_ref[p, 0:GROUP, :] for p in places], axis=0)
    gt = jnp.concatenate([recv_ref[p, GROUP : 2 * GROUP, :] for p in places], axis=0)
    own = lax.axis_index("seq")
    taps = filters_ref[...].astype(F32)
    which = lax.broadcasted_iota(jnp.int32, taps.shape, 0)
    row = jnp.sum(jnp.where(which == own, taps, 0.0), axis=0, keepdims=True)
    padded = jnp.concatenate([jnp.zeros((1, width), F32), row], axis=1)
    toep = pltpu.roll(
        jnp.broadcast_to(padded, (width, length + width)), 0, 1, stride=1, stride_axis=0
    ).astype(BF16)

    at = lax.broadcasted_iota(jnp.int32, (width, width), 0)
    to = lax.broadcasted_iota(jnp.int32, (width, width), 1)
    flip = jnp.where(at + to == width - 1, 1.0, 0.0).astype(BF16)
    x_rev = lax.dot_general(
        flip, xt, (((1,), (1,)), ((), ())), preferred_element_type=F32
    ).astype(BF16)
    gt_pad = jnp.concatenate([gt, jnp.zeros((rows, width), BF16)], axis=0)
    pairs = [
        jnp.dot(
            x_rev,
            jnp.concatenate(
                [gt_pad[GROUP * d : GROUP * d + rows], gt_pad[GROUP * (d + 1) : GROUP * (d + 1) + rows]],
                axis=1,
            ),
            preferred_element_type=F32,
        )
        for d in range(0, blocks, 2)
    ]
    pairs = jnp.concatenate(pairs + [jnp.zeros((width, width), F32)], axis=1)
    turned = pltpu.roll(pairs, 1, 1, stride=1, stride_axis=0)
    lags = jnp.sum(turned[:, width:], axis=0, keepdims=True)
    high = lags.astype(BF16).astype(F32)
    terms = jnp.concatenate([high, lags - high], axis=0).astype(BF16)
    for place, i in enumerate(ORDER_OUT):
        back_ref[place, GROUP] = terms[:, width * i : width * (i + 1)]

    def wide(v):
        v = v.reshape(blocks // 2, 2, GROUP, width)
        return jnp.concatenate([v[:, 0].reshape(half, width), v[:, 1].reshape(half, width)], axis=1)

    half = rows // 2
    x2 = wide(xt)
    g2 = wide(gt)
    filt2 = None
    back2 = None
    for d in range(blocks // 2):
        top = toep[:, width * (2 * d + 1) : width * (2 * d + 3)]
        if d == 0:
            low = jnp.concatenate([jnp.zeros((width, width), BF16), toep[:, width : 2 * width]], axis=1)
        else:
            low = toep[:, width * 2 * d : width * (2 * d + 2)]
        kern = jnp.concatenate([top, low], axis=0)
        part = jnp.dot(x2[: half - GROUP * d], kern, preferred_element_type=F32)
        rev = lax.dot_general(
            g2[GROUP * d :], kern, (((1,), (1,)), ((), ())), preferred_element_type=F32
        )
        if d == 0:
            filt2, back2 = part, rev
        else:
            zeros = jnp.zeros((GROUP * d, 2 * width), F32)
            filt2 = filt2 + jnp.concatenate([zeros, part], axis=0)
            back2 = back2 + jnp.concatenate([rev, zeros], axis=0)
    filt2 = filt2.astype(BF16)
    back2 = back2.astype(BF16)
    for place, i in enumerate(ORDER_OUT):
        at = (slice(GROUP * (i // 2), GROUP * (i // 2 + 1)), slice(width * (i % 2), width * (i % 2 + 1)))
        back_ref[place, 0 : GROUP // 2] = filt2[at].reshape(GROUP // 2, 2, width)
        back_ref[place, GROUP // 2 : GROUP] = back2[at].reshape(GROUP // 2, 2, width)


def gate_kernel(length, recv_ref, post_ref, pre_ref, values_ref, gout_ref, out_ref, gpost_ref, gpre_ref, gval_ref, gfilt_ref):
    n_filters, _, _, tokens = recv_ref.shape
    places = [ORDER_OUT.index(f) for f in range(n_filters)]
    filt, back = [
        jnp.concatenate(
            [recv_ref[p, half : half + GROUP // 2].reshape(GROUP, tokens) for p in places], axis=0
        )
        .astype(F32)
        .T
        for half in (0, GROUP // 2)
    ]
    out_ref[...] = (post_ref[...].astype(F32) * filt).astype(BF16)
    gpost_ref[...] = (gout_ref[...].astype(F32) * filt).astype(BF16)
    gpre_ref[...] = (back * values_ref[...].astype(F32)).astype(BF16)
    gval_ref[...] = (back * pre_ref[...].astype(F32)).astype(BF16)
    scale = 1.0 / math.sqrt(GROUP * length)
    lags = [
        jnp.sum(recv_ref[p, GROUP].astype(F32), axis=0, keepdims=True)
        for p in places
    ]
    gfilt_ref[...] = jnp.concatenate(lags, axis=0) * scale


def on_device(post_gate, pre_gate, values_in, filters, grad_out):
    tokens, channels = post_gate.shape
    n_filters, length = filters.shape
    vmem = pl.BlockSpec(memory_space=pltpu.VMEM)
    hbm = pl.BlockSpec(memory_space=pltpu.HBM)
    send = pl.pallas_call(
        pack_kernel,
        out_shape=jax.ShapeDtypeStruct((n_filters, 2 * GROUP, tokens), BF16),
        in_specs=[hbm] * 4,
        out_specs=vmem,
        scratch_shapes=[
            pltpu.VMEM((4, tokens, channels), BF16),
            pltpu.SemaphoreType.DMA((4,)),
        ],
        compiler_params=pltpu.CompilerParams(vmem_limit_bytes=VMEM),
        name="pack",
    )(*[pltpu.with_memory_space_constraint(x, pltpu.HBM) for x in (post_gate, pre_gate, values_in, grad_out)])
    recv = lax.all_to_all(
        send, "seq", 0, 0, tiled=True, axis_index_groups=[ORDER_IN]
    )
    back = pl.pallas_call(
        conv_kernel,
        out_shape=jax.ShapeDtypeStruct((n_filters, BACK_PAIRS, 2, tokens), BF16),
        in_specs=[vmem, vmem],
        out_specs=vmem,
        compiler_params=pltpu.CompilerParams(vmem_limit_bytes=VMEM),
        name="conv",
    )(recv, filters)
    back = lax.all_to_all(
        back, "seq", 0, 0, tiled=True, axis_index_groups=[ORDER_OUT]
    )
    grid_out = jax.ShapeDtypeStruct((tokens, channels), BF16)
    return pl.pallas_call(
        functools.partial(gate_kernel, length),
        out_shape=(grid_out,) * 4 + (jax.ShapeDtypeStruct((n_filters, tokens), F32),),
        in_specs=[vmem] * 5,
        out_specs=(vmem,) * 5,
        compiler_params=pltpu.CompilerParams(vmem_limit_bytes=VMEM),
        name="gate",
    )(back, post_gate, pre_gate, values_in, grad_out)


def solution(mesh):
    return jax.shard_map(
        on_device,
        mesh=mesh,
        in_specs=(
            P("seq", "grp"),
            P("seq", "grp"),
            P("seq", "grp"),
            P("grp", None),
            P("seq", "grp"),
        ),
        out_specs=(
            P("seq", "grp"),
            P("seq", "grp"),
            P("seq", "grp"),
            P("seq", "grp"),
            P("grp", "seq"),
        ),
        check_vma=False,
    )
```

```python
import functools
import math

import jax
import jax.numpy as jnp
from jax import lax
from jax.experimental import pallas as pl
from jax.experimental.pallas import tpu as pltpu
from jax.sharding import PartitionSpec as P

GROUP = 16
BACK_PAIRS = GROUP + 1
F32 = jnp.float32
BF16 = jnp.bfloat16
VMEM = 8 * 1024 * 1024


ORDER_IN = [13, 14, 9, 7, 5, 3, 1, 15, 12, 10, 8, 6, 4, 2, 0, 11]
ORDER_OUT = [13, 15, 0, 2, 4, 6, 8, 10, 12, 14, 1, 3, 5, 7, 9, 11]


def pack_kernel(post_hbm, pre_hbm, values_hbm, gout_hbm, send_ref, held, sems):
    copies = [
        pltpu.make_async_copy(hbm, held.at[k], sems.at[k])
        for k, hbm in enumerate((pre_hbm, values_hbm, gout_hbm, post_hbm))
    ]
    for copy in copies:
        copy.start()
    for k in range(2):
        copies[2 * k].wait()
        copies[2 * k + 1].wait()
        product = held[2 * k].astype(F32) * held[2 * k + 1].astype(F32)
        turned = product.astype(BF16).T
        for place, f in enumerate(ORDER_IN):
            send_ref[place, GROUP * k : GROUP * (k + 1), :] = turned[GROUP * f : GROUP * (f + 1)]


def conv_kernel(recv_ref, filters_ref, back_ref):
    blocks, _, width = recv_ref.shape
    rows = blocks * GROUP
    length = blocks * width
    places = [ORDER_IN.index(block) for block in range(blocks)]
    xt = jnp.concatenate([recv_ref[p, 0:GROUP, :] for p in places], axis=0)
    gt = jnp.concatenate([recv_ref[p, GROUP : 2 * GROUP, :] for p in places], axis=0)
    own = lax.axis_index("seq")
    taps = filters_ref[...].astype(F32)
    which = lax.broadcasted_iota(jnp.int32, taps.shape, 0)
    row = jnp.sum(jnp.where(which == own, taps, 0.0), axis=0, keepdims=True)
    padded = jnp.concatenate([jnp.zeros((1, width), F32), row], axis=1)
    toep = pltpu.roll(
        jnp.broadcast_to(padded, (width, length + width)), 0, 1, stride=1, stride_axis=0
    ).astype(BF16)

    at = lax.broadcasted_iota(jnp.int32, (width, width), 0)
    to = lax.broadcasted_iota(jnp.int32, (width, width), 1)
    flip = jnp.where(at + to == width - 1, 1.0, 0.0).astype(BF16)
    x_rev = lax.dot_general(
        flip, xt, (((1,), (1,)), ((), ())), preferred_element_type=F32
    ).astype(BF16)
    gt_pad = jnp.concatenate([gt, jnp.zeros((rows, width), BF16)], axis=0)
    pairs = [
        jnp.dot(
            x_rev,
            jnp.concatenate(
                [gt_pad[GROUP * d : GROUP * d + rows], gt_pad[GROUP * (d + 1) : GROUP * (d + 1) + rows]],
                axis=1,
            ),
            preferred_element_type=F32,
        )
        for d in range(0, blocks, 2)
    ]
    pairs = jnp.concatenate(pairs + [jnp.zeros((width, width), F32)], axis=1)
    turned = pltpu.roll(pairs, 1, 1, stride=1, stride_axis=0)
    lags = jnp.sum(turned[:, width:], axis=0, keepdims=True)
    high = lags.astype(BF16).astype(F32)
    terms = jnp.concatenate([high, lags - high], axis=0).astype(BF16)
    for place, i in enumerate(ORDER_OUT):
        back_ref[place, GROUP] = terms[:, width * i : width * (i + 1)]

    def wide(v):
        v = v.reshape(blocks // 2, 2, GROUP, width)
        return jnp.concatenate([v[:, 0].reshape(half, width), v[:, 1].reshape(half, width)], axis=1)

    half = rows // 2
    x2 = wide(xt)
    g2 = wide(gt)
    kerns = []
    for d in range(blocks // 2):
        top = toep[:, width * (2 * d + 1) : width * (2 * d + 3)]
        if d == 0:
            low = jnp.concatenate([jnp.zeros((width, width), BF16), toep[:, width : 2 * width]], axis=1)
        else:
            low = toep[:, width * 2 * d : width * (2 * d + 2)]
        kerns.append(jnp.concatenate([top, low], axis=0))
    zero = jnp.zeros((half, 2 * width), BF16)
    x_pad = jnp.concatenate([zero, x2], axis=0)
    g_pad = jnp.concatenate([g2, zero], axis=0)
    x_col = jnp.concatenate([x_pad[half - GROUP * d : 2 * half - GROUP * d] for d in range(blocks // 2)], axis=1)
    g_col = jnp.concatenate([g_pad[GROUP * d : GROUP * d + half] for d in range(blocks // 2)], axis=1)
    filt2 = jnp.dot(x_col, jnp.concatenate(kerns, axis=0), preferred_element_type=F32)
    back2 = lax.dot_general(
        g_col, jnp.concatenate(kerns, axis=1), (((1,), (1,)), ((), ())), preferred_element_type=F32
    )
    filt2 = filt2.astype(BF16)
    back2 = back2.astype(BF16)
    for place, i in enumerate(ORDER_OUT):
        at = (slice(GROUP * (i // 2), GROUP * (i // 2 + 1)), slice(width * (i % 2), width * (i % 2 + 1)))
        back_ref[place, 0 : GROUP // 2] = filt2[at].reshape(GROUP // 2, 2, width)
        back_ref[place, GROUP // 2 : GROUP] = back2[at].reshape(GROUP // 2, 2, width)


def gate_kernel(length, recv_ref, post_ref, pre_ref, values_ref, gout_ref, out_ref, gpost_ref, gpre_ref, gval_ref, gfilt_ref):
    n_filters, _, _, tokens = recv_ref.shape
    places = [ORDER_OUT.index(f) for f in range(n_filters)]
    filt, back = [
        jnp.concatenate(
            [recv_ref[p, half : half + GROUP // 2].reshape(GROUP, tokens) for p in places], axis=0
        )
        .T.astype(F32)
        for half in (0, GROUP // 2)
    ]
    out_ref[...] = (post_ref[...].astype(F32) * filt).astype(BF16)
    gpost_ref[...] = (gout_ref[...].astype(F32) * filt).astype(BF16)
    gpre_ref[...] = (back * values_ref[...].astype(F32)).astype(BF16)
    gval_ref[...] = (back * pre_ref[...].astype(F32)).astype(BF16)
    scale = 1.0 / math.sqrt(GROUP * length)
    lags = [
        jnp.sum(recv_ref[p, GROUP].astype(F32), axis=0, keepdims=True)
        for p in places
    ]
    gfilt_ref[...] = jnp.concatenate(lags, axis=0) * scale


def on_device(post_gate, pre_gate, values_in, filters, grad_out):
    tokens, channels = post_gate.shape
    n_filters, length = filters.shape
    vmem = pl.BlockSpec(memory_space=pltpu.VMEM)
    hbm = pl.BlockSpec(memory_space=pltpu.HBM)
    send = pl.pallas_call(
        pack_kernel,
        out_shape=jax.ShapeDtypeStruct((n_filters, 2 * GROUP, tokens), BF16),
        in_specs=[hbm] * 4,
        out_specs=vmem,
        scratch_shapes=[
            pltpu.VMEM((4, tokens, channels), BF16),
            pltpu.SemaphoreType.DMA((4,)),
        ],
        compiler_params=pltpu.CompilerParams(vmem_limit_bytes=VMEM),
        name="pack",
    )(*[pltpu.with_memory_space_constraint(x, pltpu.HBM) for x in (post_gate, pre_gate, values_in, grad_out)])
    recv = lax.all_to_all(
        send, "seq", 0, 0, tiled=True, axis_index_groups=[ORDER_IN]
    )
    back = pl.pallas_call(
        conv_kernel,
        out_shape=jax.ShapeDtypeStruct((n_filters, BACK_PAIRS, 2, tokens), BF16),
        in_specs=[vmem, vmem],
        out_specs=vmem,
        compiler_params=pltpu.CompilerParams(vmem_limit_bytes=VMEM),
        name="conv",
    )(recv, filters)
    back = lax.all_to_all(
        back, "seq", 0, 0, tiled=True, axis_index_groups=[ORDER_OUT]
    )
    grid_out = jax.ShapeDtypeStruct((tokens, channels), BF16)
    return pl.pallas_call(
        functools.partial(gate_kernel, length),
        out_shape=(grid_out,) * 4 + (jax.ShapeDtypeStruct((n_filters, tokens), F32),),
        in_specs=[vmem] * 5,
        out_specs=(vmem,) * 5,
        compiler_params=pltpu.CompilerParams(vmem_limit_bytes=VMEM),
        name="gate",
    )(back, post_gate, pre_gate, values_in, grad_out)


def solution(mesh):
    return jax.shard_map(
        on_device,
        mesh=mesh,
        in_specs=(
            P("seq", "grp"),
            P("seq", "grp"),
            P("seq", "grp"),
            P("grp", None),
            P("seq", "grp"),
        ),
        out_specs=(
            P("seq", "grp"),
            P("seq", "grp"),
            P("seq", "grp"),
            P("seq", "grp"),
            P("grp", "seq"),
        ),
        check_vma=False,
    )
```

```python
import functools
import math

import jax
import jax.numpy as jnp
from jax import lax
from jax.experimental import pallas as pl
from jax.experimental.pallas import tpu as pltpu
from jax.sharding import PartitionSpec as P

GROUP = 16
BACK_PAIRS = GROUP + 1
F32 = jnp.float32
BF16 = jnp.bfloat16
VMEM = 8 * 1024 * 1024


ORDER_IN = [13, 14, 9, 7, 5, 3, 1, 15, 12, 10, 8, 6, 4, 2, 0, 11]
ORDER_OUT = [13, 15, 0, 2, 4, 6, 8, 10, 12, 14, 1, 3, 5, 7, 9, 11]


def pack_kernel(post_hbm, pre_hbm, values_hbm, gout_hbm, send_ref, held, sems):
    copies = [
        pltpu.make_async_copy(hbm, held.at[k], sems.at[k])
        for k, hbm in enumerate((pre_hbm, values_hbm, gout_hbm, post_hbm))
    ]
    for copy in copies:
        copy.start()
    for k in range(2):
        copies[2 * k].wait()
        copies[2 * k + 1].wait()
        product = held[2 * k].astype(F32) * held[2 * k + 1].astype(F32)
        turned = product.astype(BF16).T
        for place, f in enumerate(ORDER_IN):
            send_ref[place, GROUP * k : GROUP * (k + 1), :] = turned[GROUP * f : GROUP * (f + 1)]


def conv_kernel(recv_ref, filters_ref, back_ref):
    blocks, _, width = recv_ref.shape
    rows = blocks * GROUP
    length = blocks * width
    places = [ORDER_IN.index(block) for block in range(blocks)]
    xt = jnp.concatenate([recv_ref[p, 0:GROUP, :] for p in places], axis=0)
    gt = jnp.concatenate([recv_ref[p, GROUP : 2 * GROUP, :] for p in places], axis=0)
    own = lax.axis_index("seq")
    taps = filters_ref[...].astype(F32)
    which = lax.broadcasted_iota(jnp.int32, taps.shape, 0)
    row = jnp.sum(jnp.where(which == own, taps, 0.0), axis=0, keepdims=True)
    padded = jnp.concatenate([jnp.zeros((1, width), F32), row], axis=1)
    eight = pltpu.roll(jnp.broadcast_to(padded, (8, length + width)), 0, 1, stride=1, stride_axis=0)
    toep = jnp.concatenate(
        [eight] + [pltpu.roll(eight, 8 * q, 1) for q in range(1, width // 8)], axis=0
    ).astype(BF16)

    at = lax.broadcasted_iota(jnp.int32, (width, width), 0)
    to = lax.broadcasted_iota(jnp.int32, (width, width), 1)
    flip = jnp.where(at + to == width - 1, 1.0, 0.0).astype(BF16)
    x_rev = lax.dot_general(
        flip, xt, (((1,), (1,)), ((), ())), preferred_element_type=F32
    ).astype(BF16)
    gt_pad = jnp.concatenate([gt, jnp.zeros((rows, width), BF16)], axis=0)
    pairs = [
        jnp.dot(
            x_rev,
            jnp.concatenate(
                [gt_pad[GROUP * d : GROUP * d + rows], gt_pad[GROUP * (d + 1) : GROUP * (d + 1) + rows]],
                axis=1,
            ),
            preferred_element_type=F32,
        )
        for d in range(0, blocks, 2)
    ]
    pairs = jnp.concatenate(pairs + [jnp.zeros((width, width), F32)], axis=1)
    turned = pltpu.roll(pairs, 1, 1, stride=1, stride_axis=0)
    lags = jnp.sum(turned[:, width:], axis=0, keepdims=True)
    high = lags.astype(BF16).astype(F32)
    terms = jnp.concatenate([high, lags - high], axis=0).astype(BF16)
    for place, i in enumerate(ORDER_OUT):
        back_ref[place, GROUP] = terms[:, width * i : width * (i + 1)]

    filt = None
    back = None
    for d in range(0, blocks, 2):
        kern = toep[:, width * (d + 1) : width * (d + 3)]
        keep = rows - GROUP * d
        part = jnp.dot(xt[:keep], kern, preferred_element_type=F32)
        near = part[:, :width]
        far = part[: keep - GROUP, width:]
        grads = jnp.concatenate(
            [gt_pad[GROUP * d : rows], gt_pad[GROUP * (d + 1) : rows + GROUP]], axis=1
        )
        rev = lax.dot_general(
            grads, kern, (((1,), (1,)), ((), ())), preferred_element_type=F32
        )
        if d == 0:
            filt = near + jnp.concatenate([jnp.zeros((GROUP, width), F32), far], axis=0)
            back = rev
        else:
            zeros = jnp.zeros((GROUP * d, width), F32)
            more = jnp.zeros((GROUP * (d + 1), width), F32)
            filt = filt + jnp.concatenate([zeros, near], axis=0) + jnp.concatenate([more, far], axis=0)
            back = back + jnp.concatenate([rev, zeros], axis=0)
    filt = filt.astype(BF16)
    back = back.astype(BF16)
    for place, i in enumerate(ORDER_OUT):
        at = slice(GROUP * i, GROUP * (i + 1))
        back_ref[place, 0 : GROUP // 2] = filt[at].reshape(GROUP // 2, 2, width)
        back_ref[place, GROUP // 2 : GROUP] = back[at].reshape(GROUP // 2, 2, width)


def gate_kernel(length, recv_ref, post_ref, pre_ref, values_ref, gout_ref, out_ref, gpost_ref, gpre_ref, gval_ref, gfilt_ref):
    n_filters, _, _, tokens = recv_ref.shape
    places = [ORDER_OUT.index(f) for f in range(n_filters)]
    filt, back = [
        jnp.concatenate(
            [recv_ref[p, half : half + GROUP // 2].reshape(GROUP, tokens) for p in places], axis=0
        )
        .T.astype(F32)
        for half in (0, GROUP // 2)
    ]
    out_ref[...] = (post_ref[...].astype(F32) * filt).astype(BF16)
    gpost_ref[...] = (gout_ref[...].astype(F32) * filt).astype(BF16)
    gpre_ref[...] = (back * values_ref[...].astype(F32)).astype(BF16)
    gval_ref[...] = (back * pre_ref[...].astype(F32)).astype(BF16)
    scale = 1.0 / math.sqrt(GROUP * length)
    lags = [
        jnp.sum(recv_ref[p, GROUP].astype(F32), axis=0, keepdims=True)
        for p in places
    ]
    gfilt_ref[...] = jnp.concatenate(lags, axis=0) * scale


def on_device(post_gate, pre_gate, values_in, filters, grad_out):
    tokens, channels = post_gate.shape
    n_filters, length = filters.shape
    vmem = pl.BlockSpec(memory_space=pltpu.VMEM)
    hbm = pl.BlockSpec(memory_space=pltpu.HBM)
    send = pl.pallas_call(
        pack_kernel,
        out_shape=jax.ShapeDtypeStruct((n_filters, 2 * GROUP, tokens), BF16),
        in_specs=[hbm] * 4,
        out_specs=vmem,
        scratch_shapes=[
            pltpu.VMEM((4, tokens, channels), BF16),
            pltpu.SemaphoreType.DMA((4,)),
        ],
        compiler_params=pltpu.CompilerParams(vmem_limit_bytes=VMEM),
        name="pack",
    )(*[pltpu.with_memory_space_constraint(x, pltpu.HBM) for x in (post_gate, pre_gate, values_in, grad_out)])
    recv = lax.all_to_all(
        send, "seq", 0, 0, tiled=True, axis_index_groups=[ORDER_IN]
    )
    back = pl.pallas_call(
        conv_kernel,
        out_shape=jax.ShapeDtypeStruct((n_filters, BACK_PAIRS, 2, tokens), BF16),
        in_specs=[vmem, vmem],
        out_specs=vmem,
        compiler_params=pltpu.CompilerParams(vmem_limit_bytes=VMEM),
        name="conv",
    )(recv, filters)
    back = lax.all_to_all(
        back, "seq", 0, 0, tiled=True, axis_index_groups=[ORDER_OUT]
    )
    grid_out = jax.ShapeDtypeStruct((tokens, channels), BF16)
    return pl.pallas_call(
        functools.partial(gate_kernel, length),
        out_shape=(grid_out,) * 4 + (jax.ShapeDtypeStruct((n_filters, tokens), F32),),
        in_specs=[vmem] * 5,
        out_specs=(vmem,) * 5,
        compiler_params=pltpu.CompilerParams(vmem_limit_bytes=VMEM),
        name="gate",
    )(back, post_gate, pre_gate, values_in, grad_out)


def solution(mesh):
    return jax.shard_map(
        on_device,
        mesh=mesh,
        in_specs=(
            P("seq", "grp"),
            P("seq", "grp"),
            P("seq", "grp"),
            P("grp", None),
            P("seq", "grp"),
        ),
        out_specs=(
            P("seq", "grp"),
            P("seq", "grp"),
            P("seq", "grp"),
            P("seq", "grp"),
            P("grp", "seq"),
        ),
        check_vma=False,
    )
```

```python
import functools
import math

import jax
import jax.numpy as jnp
from jax import lax
from jax.experimental import pallas as pl
from jax.experimental.pallas import tpu as pltpu
from jax.sharding import PartitionSpec as P

GROUP = 16
BACK_PAIRS = GROUP + 1
F32 = jnp.float32
BF16 = jnp.bfloat16
VMEM = 8 * 1024 * 1024


ORDER_IN = [13, 14, 9, 7, 5, 3, 0, 15, 12, 10, 8, 6, 4, 2, 1, 11]
ORDER_OUT = [13, 15, 0, 2, 4, 6, 8, 10, 12, 14, 1, 3, 5, 7, 9, 11]


def pack_kernel(post_hbm, pre_hbm, values_hbm, gout_hbm, send_ref, held, sems):
    copies = [
        pltpu.make_async_copy(hbm, held.at[k], sems.at[k])
        for k, hbm in enumerate((pre_hbm, values_hbm, gout_hbm, post_hbm))
    ]
    for copy in copies:
        copy.start()
    for k in range(2):
        copies[2 * k].wait()
        copies[2 * k + 1].wait()
        product = held[2 * k].astype(F32) * held[2 * k + 1].astype(F32)
        turned = product.astype(BF16).T
        for place, f in enumerate(ORDER_IN):
            send_ref[place, GROUP * k : GROUP * (k + 1), :] = turned[GROUP * f : GROUP * (f + 1)]


def conv_kernel(recv_ref, filters_ref, back_ref):
    blocks, _, width = recv_ref.shape
    rows = blocks * GROUP
    length = blocks * width
    places = [ORDER_IN.index(block) for block in range(blocks)]
    xt = jnp.concatenate([recv_ref[p, 0:GROUP, :] for p in places], axis=0)
    gt = jnp.concatenate([recv_ref[p, GROUP : 2 * GROUP, :] for p in places], axis=0)
    own = lax.axis_index("seq")
    taps = filters_ref[...].astype(F32)
    which = lax.broadcasted_iota(jnp.int32, taps.shape, 0)
    row = jnp.sum(jnp.where(which == own, taps, 0.0), axis=0, keepdims=True)
    padded = jnp.concatenate([jnp.zeros((1, width), F32), row], axis=1)
    eight = pltpu.roll(jnp.broadcast_to(padded, (8, length + width)), 0, 1, stride=1, stride_axis=0)
    toep = jnp.concatenate(
        [eight] + [pltpu.roll(eight, 8 * q, 1) for q in range(1, width // 8)], axis=0
    ).astype(BF16)

    at = lax.broadcasted_iota(jnp.int32, (width, width), 0)
    to = lax.broadcasted_iota(jnp.int32, (width, width), 1)
    flip = jnp.where(at + to == width - 1, 1.0, 0.0).astype(BF16)
    x_rev = lax.dot_general(
        flip, xt, (((1,), (1,)), ((), ())), preferred_element_type=F32
    ).astype(BF16)
    gt_pad = jnp.concatenate([gt, jnp.zeros((rows, width), BF16)], axis=0)
    pairs = [
        jnp.dot(
            x_rev,
            jnp.concatenate(
                [gt_pad[GROUP * d : GROUP * d + rows], gt_pad[GROUP * (d + 1) : GROUP * (d + 1) + rows]],
                axis=1,
            ),
            preferred_element_type=F32,
        )
        for d in range(0, blocks, 2)
    ]
    pairs = jnp.concatenate(pairs + [jnp.zeros((width, width), F32)], axis=1)
    turned = pltpu.roll(pairs, 1, 1, stride=1, stride_axis=0)
    lags = jnp.sum(turned[:, width:], axis=0, keepdims=True)
    high = lags.astype(BF16).astype(F32)
    terms = jnp.concatenate([high, lags - high], axis=0).astype(BF16)
    for place, i in enumerate(ORDER_OUT):
        back_ref[place, GROUP] = terms[:, width * i : width * (i + 1)]

    filt = None
    back = None
    for d in range(0, blocks, 2):
        kern = toep[:, width * (d + 1) : width * (d + 3)]
        keep = rows - GROUP * d
        part = jnp.dot(xt[:keep], kern, preferred_element_type=F32)
        near = part[:, :width]
        far = part[: keep - GROUP, width:]
        grads = jnp.concatenate(
            [gt_pad[GROUP * d : rows], gt_pad[GROUP * (d + 1) : rows + GROUP]], axis=1
        )
        rev = lax.dot_general(
            grads, kern, (((1,), (1,)), ((), ())), preferred_element_type=F32
        )
        if d == 0:
            filt = near + jnp.concatenate([jnp.zeros((GROUP, width), F32), far], axis=0)
            back = rev
        else:
            zeros = jnp.zeros((GROUP * d, width), F32)
            more = jnp.zeros((GROUP * (d + 1), width), F32)
            filt = filt + jnp.concatenate([zeros, near], axis=0) + jnp.concatenate([more, far], axis=0)
            back = back + jnp.concatenate([rev, zeros], axis=0)
    filt = filt.astype(BF16)
    back = back.astype(BF16)
    for place, i in enumerate(ORDER_OUT):
        at = slice(GROUP * i, GROUP * (i + 1))
        back_ref[place, 0 : GROUP // 2] = filt[at].reshape(GROUP // 2, 2, width)
        back_ref[place, GROUP // 2 : GROUP] = back[at].reshape(GROUP // 2, 2, width)


def gate_kernel(length, recv_ref, post_ref, pre_ref, values_ref, gout_ref, out_ref, gpost_ref, gpre_ref, gval_ref, gfilt_ref):
    n_filters, _, _, tokens = recv_ref.shape
    places = [ORDER_OUT.index(f) for f in range(n_filters)]
    filt, back = [
        jnp.concatenate(
            [recv_ref[p, half : half + GROUP // 2].reshape(GROUP, tokens) for p in places], axis=0
        )
        .T.astype(F32)
        for half in (0, GROUP // 2)
    ]
    out_ref[...] = (post_ref[...].astype(F32) * filt).astype(BF16)
    gpost_ref[...] = (gout_ref[...].astype(F32) * filt).astype(BF16)
    gpre_ref[...] = (back * values_ref[...].astype(F32)).astype(BF16)
    gval_ref[...] = (back * pre_ref[...].astype(F32)).astype(BF16)
    scale = 1.0 / math.sqrt(GROUP * length)
    lags = [
        jnp.sum(recv_ref[p, GROUP].astype(F32), axis=0, keepdims=True)
        for p in places
    ]
    gfilt_ref[...] = jnp.concatenate(lags, axis=0) * scale


def on_device(post_gate, pre_gate, values_in, filters, grad_out):
    tokens, channels = post_gate.shape
    n_filters, length = filters.shape
    vmem = pl.BlockSpec(memory_space=pltpu.VMEM)
    hbm = pl.BlockSpec(memory_space=pltpu.HBM)
    send = pl.pallas_call(
        pack_kernel,
        out_shape=jax.ShapeDtypeStruct((n_filters, 2 * GROUP, tokens), BF16),
        in_specs=[hbm] * 4,
        out_specs=vmem,
        scratch_shapes=[
            pltpu.VMEM((4, tokens, channels), BF16),
            pltpu.SemaphoreType.DMA((4,)),
        ],
        compiler_params=pltpu.CompilerParams(vmem_limit_bytes=VMEM),
        name="pack",
    )(*[pltpu.with_memory_space_constraint(x, pltpu.HBM) for x in (post_gate, pre_gate, values_in, grad_out)])
    recv = lax.all_to_all(
        send, "seq", 0, 0, tiled=True, axis_index_groups=[ORDER_IN]
    )
    back = pl.pallas_call(
        conv_kernel,
        out_shape=jax.ShapeDtypeStruct((n_filters, BACK_PAIRS, 2, tokens), BF16),
        in_specs=[vmem, vmem],
        out_specs=vmem,
        compiler_params=pltpu.CompilerParams(vmem_limit_bytes=VMEM),
        name="conv",
    )(recv, filters)
    back = lax.all_to_all(
        back, "seq", 0, 0, tiled=True, axis_index_groups=[ORDER_OUT]
    )
    grid_out = jax.ShapeDtypeStruct((tokens, channels), BF16)
    return pl.pallas_call(
        functools.partial(gate_kernel, length),
        out_shape=(grid_out,) * 4 + (jax.ShapeDtypeStruct((n_filters, tokens), F32),),
        in_specs=[vmem] * 5,
        out_specs=(vmem,) * 5,
        compiler_params=pltpu.CompilerParams(vmem_limit_bytes=VMEM),
        name="gate",
    )(back, post_gate, pre_gate, values_in, grad_out)


def solution(mesh):
    return jax.shard_map(
        on_device,
        mesh=mesh,
        in_specs=(
            P("seq", "grp"),
            P("seq", "grp"),
            P("seq", "grp"),
            P("grp", None),
            P("seq", "grp"),
        ),
        out_specs=(
            P("seq", "grp"),
            P("seq", "grp"),
            P("seq", "grp"),
            P("seq", "grp"),
            P("grp", "seq"),
        ),
        check_vma=False,
    )
```
